32 devices in a mesh: groups: 2 (over y), wloop: 4 (over z), items: 4 (over x, core).
Axes of the slice: x: 2, y: 2, z: 4, core: 2. Of those that a mesh axis runs over, the one named last changes fastest.
Arguments:
- features: bfloat16 [2048, 16384], P(('groups', 'items'), 'wloop'), parts along dimension 0, may hold values from -6 to 6
- cotangent: bfloat16 [2048, 16384], P(('groups', 'items'), 'wloop'), parts along dimension 0, may hold values from -6 to 6
- block_weights: bfloat16 [256, 256, 256], P('wloop'), may hold values from -0.1875 to 0.1875
- block_rows: int32 [256], P('wloop'), may hold values from 0 to 63, as said below
- block_cols: int32 [256], P('wloop'), may hold values from 0 to 63, as said below
- lowrank_in: bfloat16 [128, 16384], P(None, 'wloop'), may hold values from -0.046875 to 0.046875
- lowrank_out: bfloat16 [128, 16384], P(None, 'wloop'), may hold values from -0.5 to 0.5
Outputs:
- mixed: bfloat16 [2048, 16384], P(('groups', 'items'), 'wloop'), parts along dimension 0
- block_grads: float32 [512, 256, 256], P(('groups', 'items'), 'wloop'), parts along dimension 0
- grad_in: float32 [256, 16384], P(('groups', 'items'), 'wloop'), parts along dimension 0
- grad_out: float32 [256, 16384], P(('groups', 'items'), 'wloop'), parts along dimension 0
The draws below stay inside these ranges and needn't reach their ends.
There are 2 independent parts, one for each index of `groups`. The reference program is written for one: setup_inputs(seed, part) draws one part's arguments, and reference() takes and returns one part's arrays. A program takes and returns all parts, laid end to end along the dimension named above; an argument that names none is the same for every part. Nothing has to cross between parts.
Inputs may be any that keep to these rules, and one draw needn't show every extreme that they name: `block_rows`: the stored blocks form a strided block pattern: every input block column c appears in exactly 4 stored blocks, whose output blocks are c, c xor 1, c xor (16) and c xor (32); the stored blocks on one index of wloop are exactly those of its 16 input block columns, in an order drawn afresh. `block_cols`: the input block column of each stored block, as described for block_rows; the stored blocks on one index of wloop have input columns within that index's range of 16 columns.
All inputs are finite; a program needn't handle non-finite values.
Results may differ from the reference program's by a relative error of at most 0.0039.
Values may be sent and summed in bfloat16 or wider, within the bound.
A program may use at most 128 MiB of HBM per device.

```python
import jax
import jax.numpy as jnp
from jax import lax

WIDTH = 16384
BLOCK = 256
LOWRANK = 128
PER_COLUMN = 4
ITEMS = 1024
STORED = 256
N_WLOOP = 4


def pattern_lists(key):
    count = WIDTH // BLOCK
    share = count // N_WLOOP
    local = PER_COLUMN * share
    keys = jax.random.split(jax.random.fold_in(key, 7), N_WLOOP)
    orders = jax.vmap(lambda one: jax.random.permutation(one, local))(keys).astype(jnp.int32)
    device = jnp.arange(N_WLOOP, dtype=jnp.int32)[:, None]
    columns = device * share + orders // PER_COLUMN
    table = jnp.array([0, 1, count // 4, count // 2], jnp.int32)
    strides = table[orders % PER_COLUMN]
    outputs = jnp.bitwise_xor(columns, strides)
    return (outputs.reshape(-1).astype(jnp.int32), columns.reshape(-1).astype(jnp.int32))


def draw_block_rows(key, part):
    return pattern_lists(key)[0]


def draw_block_cols(key, part):
    return pattern_lists(key)[1]


def shard_levels(stream_key, dims, cuts, least, largest):
    def one(dim, blocks):
        draws = jax.random.uniform(jax.random.fold_in(jax.random.fold_in(stream_key, 6), dim), (blocks,), jnp.float32, least / len(cuts), largest / len(cuts))
        return jnp.repeat(jnp.exp(draws), dims[dim] // blocks).reshape((-1,) + (1,) * (len(dims) - dim - 1))

    loudness = one(*cuts[0])
    for cut in cuts[1:]:
        loudness = loudness * one(*cut)
    return loudness


def centred(own_key, extent, scale, limit, cuts=(), held_as=jnp.bfloat16):
    result = scale * jax.random.normal(own_key, extent, jnp.float32)
    if cuts:
        result = result * shard_levels(own_key, extent, cuts, -0.22, 0.18)
    return jnp.clip(result, -limit, limit).astype(held_as)


def setup_inputs(seed: int = 0, part: int = 0) -> dict:
    splits = jax.random.split(jax.random.key(seed), 8)
    part_keys = jax.random.split(jax.random.fold_in(splits[7], part), 8)
    features = centred(part_keys[0], (ITEMS, WIDTH), 1.0, 6.0, ((0, 4), (1, 4)))
    cotangent = centred(part_keys[1], (ITEMS, WIDTH), 1.0, 6.0, ((0, 4), (1, 4)))
    block_weights = centred(splits[2], (STORED, BLOCK, BLOCK), (PER_COLUMN * BLOCK) ** -0.5, 0.1875, ((0, 4),))
    block_rows = draw_block_rows(jax.random.fold_in(splits[7], 71), part)
    block_cols = draw_block_cols(jax.random.fold_in(splits[7], 71), part)
    lowrank_in = centred(splits[5], (LOWRANK, WIDTH), WIDTH ** -0.5, 0.046875, ((1, 4),))
    lowrank_out = centred(splits[6], (LOWRANK, WIDTH), LOWRANK ** -0.5, 0.5, ((1, 4),))
    return {"features": features, "cotangent": cotangent, "block_weights": block_weights, "block_rows": block_rows, "block_cols": block_cols, "lowrank_in": lowrank_in, "lowrank_out": lowrank_out}


def reference(features, cotangent, block_weights, block_rows, block_cols, lowrank_in, lowrank_out):
    def step(total, inputs):
        weight, row, col = inputs
        start_in = (col * BLOCK).astype(jnp.int32)
        start_out = (row * BLOCK).astype(jnp.int32)
        taken = lax.dynamic_slice_in_dim(features, start_in, BLOCK, 1)
        grads = lax.dynamic_slice_in_dim(cotangent, start_out, BLOCK, 1)
        contrib = jnp.dot(taken, weight.T, preferred_element_type=jnp.float32)
        current = lax.dynamic_slice_in_dim(total, start_out, BLOCK, 1)
        total = lax.dynamic_update_slice_in_dim(total, current + contrib, start_out, 1)
        grad = jnp.dot(grads.T, taken, preferred_element_type=jnp.float32)
        return total, grad

    start = jnp.zeros((features.shape[0], WIDTH), jnp.float32)
    sparse, grads = lax.scan(step, start, (block_weights, block_rows.astype(jnp.int32), block_cols.astype(jnp.int32)))
    codes = jnp.dot(features, lowrank_in.T, preferred_element_type=jnp.float32).astype(jnp.bfloat16)
    backs = jnp.dot(cotangent, lowrank_out.T, preferred_element_type=jnp.float32).astype(jnp.bfloat16)
    mixed = (sparse + jnp.dot(codes, lowrank_out, preferred_element_type=jnp.float32)).astype(jnp.bfloat16)
    block_grads = jnp.transpose(grads, (1, 0, 2))
    grad_in = jnp.dot(backs.T, features, preferred_element_type=jnp.float32)
    grad_out = jnp.dot(codes.T, cotangent, preferred_element_type=jnp.float32)
    return mixed, block_grads, grad_in, grad_out
```

```python
import functools

import jax
import jax.numpy as jnp
from jax import lax
from jax.experimental import pallas as pl
from jax.experimental.pallas import tpu as pltpu
from jax.sharding import PartitionSpec as P

WIDTH = 16384
BLOCK = 256
LOWRANK = 128
F32 = jnp.float32
BF16 = jnp.bfloat16
NT = (((1,), (1,)), ((), ()))
TN = (((0,), (0,)), ((), ()))


def dot(a, b, dims=(((1,), (0,)), ((), ()))):
    return lax.dot_general(a, b, dims, preferred_element_type=F32)


def cost(flops, bytes_accessed):
    return pl.CostEstimate(flops=int(flops), bytes_accessed=int(bytes_accessed), transcendentals=0)


def params():
    return pltpu.CompilerParams(vmem_limit_bytes=40 << 20)


def swapped(block, axis, apart):
    count = lax.axis_size(axis)
    route = []
    for low in range(count):
        high = low | 1 << apart
        if high != low and high < count:
            route += [(low, high), (high, low)]
    return lax.ppermute(block, axis, route)


def column(rows):
    return pl.BlockSpec((rows, BLOCK), lambda j, *_: (0, j))


def paired(rows):
    return pl.BlockSpec((rows, BLOCK), lambda j, *_: (0, j + 1 - 2 * (j % 2)))


def stored(stride, flip=False):
    def place(j, table):
        if flip:
            j = j + 1 - 2 * (j % 2)
        return (table[stride, j], 0, 0)

    return pl.BlockSpec((1, BLOCK, BLOCK), place)


def far_kernel(table, x, wa, wb, oa, ob):
    oa[...] = dot(x[...], wa[0], NT).astype(BF16)
    ob[...] = dot(x[...], wb[0], NT).astype(BF16)


def far_partials(table, features, weights):
    rows, width = features.shape
    return pl.pallas_call(
        far_kernel,
        out_shape=[jax.ShapeDtypeStruct((rows, width), BF16)] * 2,
        grid_spec=pltpu.PrefetchScalarGridSpec(
            num_scalar_prefetch=1,
            grid=(width // BLOCK,),
            in_specs=[column(rows), stored(2), stored(3)],
            out_specs=[column(rows)] * 2,
        ),
        compiler_params=params(),
        cost_estimate=cost(4 * rows * width * BLOCK, 6 * rows * width + 4 * width * BLOCK),
    )(table, features, weights, weights)


def near_kernel(table, x, y, wa, wb, c, low, o):
    o[...] = dot(x[...], wa[0], NT) + dot(y[...], wb[0], NT) + dot(c[...], low[...])


def near_total(table, features, weights, codes, lowrank_out):
    rows, width = features.shape
    return pl.pallas_call(
        near_kernel,
        out_shape=jax.ShapeDtypeStruct((rows, width), F32),
        grid_spec=pltpu.PrefetchScalarGridSpec(
            num_scalar_prefetch=1,
            grid=(width // BLOCK,),
            in_specs=[
                column(rows),
                paired(rows),
                stored(0),
                stored(1, True),
                pl.BlockSpec((rows, LOWRANK), lambda j, *_: (0, 0)),
                column(LOWRANK),
            ],
            out_specs=column(rows),
        ),
        compiler_params=params(),
        cost_estimate=cost(4 * rows * width * BLOCK, 8 * rows * width + 4 * width * BLOCK),
    )(table, features, features, weights, weights, codes, lowrank_out)


def near_grad_kernel(n, x, g, h, o):
    part = BLOCK // n
    o[:, 0, 0] = dot(g[...], x[...], TN).reshape(n, part, BLOCK)
    o[:, 0, 1] = dot(h[...], x[...], TN).reshape(n, part, BLOCK)


def near_grads(n, features, cotangent):
    rows, width = features.shape
    share = width // BLOCK
    return pl.pallas_call(
        functools.partial(near_grad_kernel, n),
        grid=(share,),
        out_shape=jax.ShapeDtypeStruct((n, share, 2, BLOCK // n, BLOCK), F32),
        in_specs=[column(rows), column(rows), paired(rows)],
        out_specs=pl.BlockSpec((n, 1, 2, BLOCK // n, BLOCK), lambda j: (0, j, 0, 0, 0)),
        compiler_params=params(),
        cost_estimate=cost(4 * rows * width * BLOCK, 6 * rows * width + 8 * width * BLOCK),
    )(features, cotangent, cotangent)


def far_grad_kernel(n, x, g, ga, gb, codes, backs, o):
    part = BLOCK // n
    half = part // 2
    o[:, 0, 0] = dot(ga[...], x[...], TN).reshape(n, part, BLOCK)
    o[:, 0, 1] = dot(gb[...], x[...], TN).reshape(n, part, BLOCK)
    o[:, 0, 2, :half] = dot(backs[...], x[...], TN).reshape(n, half, BLOCK)
    o[:, 0, 2, half:] = dot(codes[...], g[...], TN).reshape(n, half, BLOCK)


def far_grads(n, features, cotangent, from_a, from_b, codes, backs):
    rows, width = features.shape
    share = width // BLOCK
    whole = pl.BlockSpec((rows, LOWRANK), lambda j: (0, 0))
    return pl.pallas_call(
        functools.partial(far_grad_kernel, n),
        grid=(share,),
        out_shape=jax.ShapeDtypeStruct((n, share, 3, BLOCK // n, BLOCK), F32),
        in_specs=[column(rows)] * 4 + [whole] * 2,
        out_specs=pl.BlockSpec((n, 1, 3, BLOCK // n, BLOCK), lambda j: (0, j, 0, 0, 0)),
        compiler_params=params(),
        cost_estimate=cost(6 * rows * width * BLOCK, 8 * rows * width + 12 * width * BLOCK),
    )(features, cotangent, from_a, from_b, codes, backs)


def place_kernel(share, table, near, far, blocks, grad_in, grad_out):
    half = grad_in.shape[0]
    for j in range(share):
        for s in range(4):
            value = near[j, s] if s < 2 else far[j, s - 2]
            blocks[:, pl.ds(table[s, j], 1), :] = value[:, None, :]
        grad_in[:, j * BLOCK : (j + 1) * BLOCK] = far[j, 2, :half]
        grad_out[:, j * BLOCK : (j + 1) * BLOCK] = far[j, 2, half:]


def place(table, near, far):
    share, _, part, _ = near.shape
    vmem = pl.BlockSpec(memory_space=pltpu.VMEM)
    return pl.pallas_call(
        functools.partial(place_kernel, share),
        out_shape=[
            jax.ShapeDtypeStruct((part, 4 * share, BLOCK), F32),
            jax.ShapeDtypeStruct((part // 2, share * BLOCK), F32),
            jax.ShapeDtypeStruct((part // 2, share * BLOCK), F32),
        ],
        in_specs=[pl.BlockSpec(memory_space=pltpu.SMEM), vmem, vmem],
        out_specs=[vmem] * 3,
        compiler_params=params(),
        cost_estimate=cost(0, 40 * share * part * BLOCK),
    )(table, near, far)


def body(features, cotangent, block_weights, block_rows, block_cols, lowrank_in, lowrank_out):
    share = features.shape[1] // BLOCK
    count = WIDTH // BLOCK
    items = lax.axis_size("items")
    top_bit = lax.axis_size("wloop").bit_length() - 1
    local_cols = block_cols % share
    stride_of = jnp.bitwise_xor(block_rows, block_cols)
    strides = jnp.array([0, 1, count // 4, count // 2], jnp.int32)
    positions = jnp.arange(share, dtype=jnp.int32)
    select = (local_cols[None, None, :] == positions[None, :, None]) & (
        stride_of[None, None, :] == strides[:, None, None]
    )
    numbers = jnp.arange(block_rows.shape[0], dtype=jnp.int32)
    table = jnp.sum(jnp.where(select, numbers[None, None, :], 0), axis=2).astype(jnp.int32)

    from_a = swapped(cotangent, "wloop", top_bit - 2)
    from_b = swapped(cotangent, "wloop", top_bit - 1)
    near = near_grads(items, features, cotangent)
    partial_code = dot(features, lowrank_in, NT)
    partial_back = dot(cotangent, lowrank_out, NT)
    codes, backs = lax.psum((partial_code, partial_back), "wloop")
    codes = codes.astype(BF16)
    backs = backs.astype(BF16)
    near_share = lax.psum_scatter(near, "items", scatter_dimension=0, tiled=True)[0]
    to_a, to_b = far_partials(table, features, block_weights)
    to_a, to_b, from_a, from_b, codes, backs = lax.optimization_barrier(
        (to_a, to_b, from_a, from_b, codes, backs)
    )
    got_a = swapped(to_a, "wloop", top_bit - 2)
    got_b = swapped(to_b, "wloop", top_bit - 1)
    far = far_grads(items, features, cotangent, from_a, from_b, codes, backs)
    far_share = lax.psum_scatter(far, "items", scatter_dimension=0, tiled=True)[0]
    total = near_total(table, features, block_weights, codes, lowrank_out)
    block_grads, grad_in, grad_out = place(table, near_share, far_share)
    mixed = (total + got_a.astype(F32) + got_b.astype(F32)).astype(BF16)
    return (mixed, block_grads, grad_in, grad_out)


def solution(mesh):
    return jax.shard_map(
        body,
        mesh=mesh,
        in_specs=(
            P(("groups", "items"), "wloop"),
            P(("groups", "items"), "wloop"),
            P("wloop", None, None),
            P("wloop"),
            P("wloop"),
            P(None, "wloop"),
            P(None, "wloop"),
        ),
        out_specs=(
            P(("groups", "items"), "wloop"),
            P(("groups", "items"), "wloop", None),
            P(("groups", "items"), "wloop"),
            P(("groups", "items"), "wloop"),
        ),
        check_vma=False,
    )
```

```python
import functools

import jax
import jax.numpy as jnp
from jax import lax
from jax.experimental import pallas as pl
from jax.experimental.pallas import tpu as pltpu
from jax.sharding import PartitionSpec as P

WIDTH = 16384
BLOCK = 256
LOWRANK = 128
F32 = jnp.float32
BF16 = jnp.bfloat16
NT = (((1,), (1,)), ((), ()))
TN = (((0,), (0,)), ((), ()))


def dot(a, b, dims=(((1,), (0,)), ((), ()))):
    return lax.dot_general(a, b, dims, preferred_element_type=F32)


def cost(flops, bytes_accessed):
    return pl.CostEstimate(flops=int(flops), bytes_accessed=int(bytes_accessed), transcendentals=0)


def params():
    return pltpu.CompilerParams(vmem_limit_bytes=40 << 20)


def swapped(block, axis, apart):
    count = lax.axis_size(axis)
    route = []
    for low in range(count):
        high = low | 1 << apart
        if high != low and high < count:
            route += [(low, high), (high, low)]
    return lax.ppermute(block, axis, route)


def column(rows):
    return pl.BlockSpec((rows, BLOCK), lambda j, *_: (0, j))


def paired(rows):
    return pl.BlockSpec((rows, BLOCK), lambda j, *_: (0, j + 1 - 2 * (j % 2)))


def stored(stride, flip=False):
    def place(j, table):
        if flip:
            j = j + 1 - 2 * (j % 2)
        return (table[stride, j], 0, 0)

    return pl.BlockSpec((1, BLOCK, BLOCK), place)


def far_kernel(table, x, wa, wb, oa, ob):
    oa[...] = dot(x[...], wa[0], NT).astype(BF16)
    ob[...] = dot(x[...], wb[0], NT).astype(BF16)


def far_partials(table, features, weights):
    rows, width = features.shape
    return pl.pallas_call(
        far_kernel,
        out_shape=[jax.ShapeDtypeStruct((rows, width), BF16)] * 2,
        grid_spec=pltpu.PrefetchScalarGridSpec(
            num_scalar_prefetch=1,
            grid=(width // BLOCK,),
            in_specs=[column(rows), stored(2), stored(3)],
            out_specs=[column(rows)] * 2,
        ),
        compiler_params=params(),
        cost_estimate=cost(4 * rows * width * BLOCK, 6 * rows * width + 4 * width * BLOCK),
    )(table, features, weights, weights)


def near_kernel(table, x, y, wa, wb, c, low, o):
    o[...] = dot(x[...], wa[0], NT) + dot(y[...], wb[0], NT) + dot(c[...], low[...])


def near_total(table, features, weights, codes, lowrank_out):
    rows, width = features.shape
    return pl.pallas_call(
        near_kernel,
        out_shape=jax.ShapeDtypeStruct((rows, width), F32),
        grid_spec=pltpu.PrefetchScalarGridSpec(
            num_scalar_prefetch=1,
            grid=(width // BLOCK,),
            in_specs=[
                column(rows),
                paired(rows),
                stored(0),
                stored(1, True),
                pl.BlockSpec((rows, LOWRANK), lambda j, *_: (0, 0)),
                column(LOWRANK),
            ],
            out_specs=column(rows),
        ),
        compiler_params=params(),
        cost_estimate=cost(4 * rows * width * BLOCK, 8 * rows * width + 4 * width * BLOCK),
    )(table, features, features, weights, weights, codes, lowrank_out)


def near_grad_kernel(n, x, g, h, o):
    part = BLOCK // n
    o[:, 0, 0] = dot(g[...], x[...], TN).reshape(n, part, BLOCK)
    o[:, 0, 1] = dot(h[...], x[...], TN).reshape(n, part, BLOCK)


def near_grads(n, features, cotangent):
    rows, width = features.shape
    share = width // BLOCK
    return pl.pallas_call(
        functools.partial(near_grad_kernel, n),
        grid=(share,),
        out_shape=jax.ShapeDtypeStruct((n, share, 2, BLOCK // n, BLOCK), F32),
        in_specs=[column(rows), column(rows), paired(rows)],
        out_specs=pl.BlockSpec((n, 1, 2, BLOCK // n, BLOCK), lambda j: (0, j, 0, 0, 0)),
        compiler_params=params(),
        cost_estimate=cost(4 * rows * width * BLOCK, 6 * rows * width + 8 * width * BLOCK),
    )(features, cotangent, cotangent)


def far_grad_kernel(n, x, g, ga, gb, codes, backs, o):
    part = BLOCK // n
    half = part // 2
    o[:, 0, 0] = dot(ga[...], x[...], TN).astype(BF16).reshape(n, part, BLOCK)
    o[:, 0, 1] = dot(gb[...], x[...], TN).astype(BF16).reshape(n, part, BLOCK)
    o[:, 0, 2, :half] = dot(backs[...], x[...], TN).astype(BF16).reshape(n, half, BLOCK)
    o[:, 0, 2, half:] = dot(codes[...], g[...], TN).astype(BF16).reshape(n, half, BLOCK)


def far_grads(n, features, cotangent, from_a, from_b, codes, backs):
    rows, width = features.shape
    share = width // BLOCK
    whole = pl.BlockSpec((rows, LOWRANK), lambda j: (0, 0))
    return pl.pallas_call(
        functools.partial(far_grad_kernel, n),
        grid=(share,),
        out_shape=jax.ShapeDtypeStruct((n, share, 3, BLOCK // n, BLOCK), BF16),
        in_specs=[column(rows)] * 4 + [whole] * 2,
        out_specs=pl.BlockSpec((n, 1, 3, BLOCK // n, BLOCK), lambda j: (0, j, 0, 0, 0)),
        compiler_params=params(),
        cost_estimate=cost(6 * rows * width * BLOCK, 8 * rows * width + 12 * width * BLOCK),
    )(features, cotangent, from_a, from_b, codes, backs)


def place_kernel(share, table, near, far, blocks, grad_in, grad_out):
    half = grad_in.shape[0]
    for j in range(share):
        for s in range(4):
            value = near[j, s] if s < 2 else far[j, s - 2].astype(F32)
            blocks[:, pl.ds(table[s, j], 1), :] = value[:, None, :]
        grad_in[:, j * BLOCK : (j + 1) * BLOCK] = far[j, 2, :half].astype(F32)
        grad_out[:, j * BLOCK : (j + 1) * BLOCK] = far[j, 2, half:].astype(F32)


def place(table, near, far):
    share, _, part, _ = near.shape
    vmem = pl.BlockSpec(memory_space=pltpu.VMEM)
    return pl.pallas_call(
        functools.partial(place_kernel, share),
        out_shape=[
            jax.ShapeDtypeStruct((part, 4 * share, BLOCK), F32),
            jax.ShapeDtypeStruct((part // 2, share * BLOCK), F32),
            jax.ShapeDtypeStruct((part // 2, share * BLOCK), F32),
        ],
        in_specs=[pl.BlockSpec(memory_space=pltpu.SMEM), vmem, vmem],
        out_specs=[vmem] * 3,
        compiler_params=params(),
        cost_estimate=cost(0, 40 * share * part * BLOCK),
    )(table, near, far)


def body(features, cotangent, block_weights, block_rows, block_cols, lowrank_in, lowrank_out):
    share = features.shape[1] // BLOCK
    count = WIDTH // BLOCK
    items = lax.axis_size("items")
    top_bit = lax.axis_size("wloop").bit_length() - 1
    local_cols = block_cols % share
    stride_of = jnp.bitwise_xor(block_rows, block_cols)
    strides = jnp.array([0, 1, count // 4, count // 2], jnp.int32)
    positions = jnp.arange(share, dtype=jnp.int32)
    select = (local_cols[None, None, :] == positions[None, :, None]) & (
        stride_of[None, None, :] == strides[:, None, None]
    )
    numbers = jnp.arange(block_rows.shape[0], dtype=jnp.int32)
    table = jnp.sum(jnp.where(select, numbers[None, None, :], 0), axis=2).astype(jnp.int32)

    from_a = swapped(cotangent, "wloop", top_bit - 2)
    from_b = swapped(cotangent, "wloop", top_bit - 1)
    to_a, to_b = far_partials(table, features, block_weights)
    near = near_grads(items, features, cotangent)
    partial_code = dot(features, lowrank_in, NT)
    partial_back = dot(cotangent, lowrank_out, NT)
    codes, backs = lax.psum((partial_code, partial_back), "wloop")
    codes = codes.astype(BF16)
    backs = backs.astype(BF16)
    near_share = lax.psum_scatter(near, "items", scatter_dimension=0, tiled=True)[0]
    to_a, to_b, from_a, from_b, codes, backs = lax.optimization_barrier(
        (to_a, to_b, from_a, from_b, codes, backs)
    )
    got_a = swapped(to_a, "wloop", top_bit - 2)
    got_b = swapped(to_b, "wloop", top_bit - 1)
    far = far_grads(items, features, cotangent, from_a, from_b, codes, backs)
    far, near_share = lax.optimization_barrier((far, near_share))
    far_share = lax.psum_scatter(far, "items", scatter_dimension=0, tiled=True)[0]
    total = near_total(table, features, block_weights, codes, lowrank_out)
    block_grads, grad_in, grad_out = place(table, near_share, far_share)
    mixed = (total + got_a.astype(F32) + got_b.astype(F32)).astype(BF16)
    return (mixed, block_grads, grad_in, grad_out)


def solution(mesh):
    return jax.shard_map(
        body,
        mesh=mesh,
        in_specs=(
            P(("groups", "items"), "wloop"),
            P(("groups", "items"), "wloop"),
            P("wloop", None, None),
            P("wloop"),
            P("wloop"),
            P(None, "wloop"),
            P(None, "wloop"),
        ),
        out_specs=(
            P(("groups", "items"), "wloop"),
            P(("groups", "items"), "wloop", None),
            P(("groups", "items"), "wloop"),
            P(("groups", "items"), "wloop"),
        ),
        check_vma=False,
    )
```

```python
import functools

import jax
import jax.numpy as jnp
from jax import lax
from jax.experimental import pallas as pl
from jax.experimental.pallas import tpu as pltpu
from jax.sharding import PartitionSpec as P

WIDTH = 16384
BLOCK = 256
LOWRANK = 128
F32 = jnp.float32
BF16 = jnp.bfloat16
NT = (((1,), (1,)), ((), ()))
TN = (((0,), (0,)), ((), ()))


def dot(a, b, dims=(((1,), (0,)), ((), ()))):
    return lax.dot_general(a, b, dims, preferred_element_type=F32)


def cost(flops, bytes_accessed):
    return pl.CostEstimate(flops=int(flops), bytes_accessed=int(bytes_accessed), transcendentals=0)


def params():
    return pltpu.CompilerParams(vmem_limit_bytes=40 << 20)


def swapped(block, axis, apart):
    count = lax.axis_size(axis)
    route = []
    for low in range(count):
        high = low | 1 << apart
        if high != low and high < count:
            route += [(low, high), (high, low)]
    return lax.ppermute(block, axis, route)


def column(rows):
    return pl.BlockSpec((rows, BLOCK), lambda j, *_: (0, j))


def paired(rows):
    return pl.BlockSpec((rows, BLOCK), lambda j, *_: (0, j + 1 - 2 * (j % 2)))


def stored(stride, flip=False):
    def place(j, table):
        if flip:
            j = j + 1 - 2 * (j % 2)
        return (table[stride, j], 0, 0)

    return pl.BlockSpec((1, BLOCK, BLOCK), place)


def far_kernel(table, x, wa, wb, oa, ob):
    oa[...] = dot(x[...], wa[0], NT).astype(BF16)
    ob[...] = dot(x[...], wb[0], NT).astype(BF16)


def far_partials(table, features, weights):
    rows, width = features.shape
    return pl.pallas_call(
        far_kernel,
        out_shape=[jax.ShapeDtypeStruct((rows, width), BF16)] * 2,
        grid_spec=pltpu.PrefetchScalarGridSpec(
            num_scalar_prefetch=1,
            grid=(width // BLOCK,),
            in_specs=[column(rows), stored(2), stored(3)],
            out_specs=[column(rows)] * 2,
        ),
        compiler_params=params(),
        cost_estimate=cost(4 * rows * width * BLOCK, 6 * rows * width + 4 * width * BLOCK),
    )(table, features, weights, weights)


def near_kernel(table, x, y, wa, wb, c, low, o):
    o[...] = dot(x[...], wa[0], NT) + dot(y[...], wb[0], NT) + dot(c[...], low[...])


def near_total(table, features, weights, codes, lowrank_out):
    rows, width = features.shape
    return pl.pallas_call(
        near_kernel,
        out_shape=jax.ShapeDtypeStruct((rows, width), F32),
        grid_spec=pltpu.PrefetchScalarGridSpec(
            num_scalar_prefetch=1,
            grid=(width // BLOCK,),
            in_specs=[
                column(rows),
                paired(rows),
                stored(0),
                stored(1, True),
                pl.BlockSpec((rows, LOWRANK), lambda j, *_: (0, 0)),
                column(LOWRANK),
            ],
            out_specs=column(rows),
        ),
        compiler_params=params(),
        cost_estimate=cost(4 * rows * width * BLOCK, 8 * rows * width + 4 * width * BLOCK),
    )(table, features, features, weights, weights, codes, lowrank_out)


def near_grad_kernel(n, table, x, g, h, o):
    part = BLOCK // n
    o[:, 0, 0] = dot(g[...], x[...], TN).reshape(n, part, BLOCK)
    o[:, 0, 1] = dot(h[...], x[...], TN).reshape(n, part, BLOCK)


def near_grads(table, n, features, cotangent):
    rows, width = features.shape
    share = width // BLOCK
    return pl.pallas_call(
        functools.partial(near_grad_kernel, n),
        grid=(share,),
        out_shape=jax.ShapeDtypeStruct((n, share, 2, BLOCK // n, BLOCK), F32),
        in_specs=[pl.BlockSpec(memory_space=pltpu.SMEM), column(rows), column(rows), paired(rows)],
        out_specs=pl.BlockSpec((n, 1, 2, BLOCK // n, BLOCK), lambda j: (0, j, 0, 0, 0)),
        compiler_params=params(),
        cost_estimate=cost(4 * rows * width * BLOCK, 6 * rows * width + 8 * width * BLOCK),
    )(table, features, cotangent, cotangent)


def far_grad_kernel(n, x, g, ga, gb, codes, backs, o):
    part = BLOCK // n
    half = part // 2
    o[:, 0, 0] = dot(ga[...], x[...], TN).astype(BF16).reshape(n, part, BLOCK)
    o[:, 0, 1] = dot(gb[...], x[...], TN).astype(BF16).reshape(n, part, BLOCK)
    o[:, 0, 2, :half] = dot(backs[...], x[...], TN).astype(BF16).reshape(n, half, BLOCK)
    o[:, 0, 2, half:] = dot(codes[...], g[...], TN).astype(BF16).reshape(n, half, BLOCK)


def far_grads(n, features, cotangent, from_a, from_b, codes, backs):
    rows, width = features.shape
    share = width // BLOCK
    whole = pl.BlockSpec((rows, LOWRANK), lambda j: (0, 0))
    return pl.pallas_call(
        functools.partial(far_grad_kernel, n),
        grid=(share,),
        out_shape=jax.ShapeDtypeStruct((n, share, 3, BLOCK // n, BLOCK), BF16),
        in_specs=[column(rows)] * 4 + [whole] * 2,
        out_specs=pl.BlockSpec((n, 1, 3, BLOCK // n, BLOCK), lambda j: (0, j, 0, 0, 0)),
        compiler_params=params(),
        cost_estimate=cost(6 * rows * width * BLOCK, 8 * rows * width + 12 * width * BLOCK),
    )(features, cotangent, from_a, from_b, codes, backs)


def place_kernel(share, table, near, far, blocks, grad_in, grad_out):
    half = grad_in.shape[0]
    for j in range(share):
        for s in range(4):
            value = near[j, s] if s < 2 else far[j, s - 2].astype(F32)
            blocks[:, pl.ds(table[s, j], 1), :] = value[:, None, :]
        grad_in[:, j * BLOCK : (j + 1) * BLOCK] = far[j, 2, :half].astype(F32)
        grad_out[:, j * BLOCK : (j + 1) * BLOCK] = far[j, 2, half:].astype(F32)


def place(table, near, far):
    share, _, part, _ = near.shape
    vmem = pl.BlockSpec(memory_space=pltpu.VMEM)
    return pl.pallas_call(
        functools.partial(place_kernel, share),
        out_shape=[
            jax.ShapeDtypeStruct((part, 4 * share, BLOCK), F32),
            jax.ShapeDtypeStruct((part // 2, share * BLOCK), F32),
            jax.ShapeDtypeStruct((part // 2, share * BLOCK), F32),
        ],
        in_specs=[pl.BlockSpec(memory_space=pltpu.SMEM), vmem, vmem],
        out_specs=[vmem] * 3,
        compiler_params=params(),
        cost_estimate=cost(0, 40 * share * part * BLOCK),
    )(table, near, far)


def body(features, cotangent, block_weights, block_rows, block_cols, lowrank_in, lowrank_out):
    share = features.shape[1] // BLOCK
    count = WIDTH // BLOCK
    items = lax.axis_size("items")
    top_bit = lax.axis_size("wloop").bit_length() - 1
    local_cols = block_cols % share
    stride_of = jnp.bitwise_xor(block_rows, block_cols)
    strides = jnp.array([0, 1, count // 4, count // 2], jnp.int32)
    positions = jnp.arange(share, dtype=jnp.int32)
    select = (local_cols[None, None, :] == positions[None, :, None]) & (
        stride_of[None, None, :] == strides[:, None, None]
    )
    numbers = jnp.arange(block_rows.shape[0], dtype=jnp.int32)
    table = jnp.sum(jnp.where(select, numbers[None, None, :], 0), axis=2).astype(jnp.int32)

    from_a = swapped(cotangent, "wloop", top_bit - 2)
    from_b = swapped(cotangent, "wloop", top_bit - 1)
    to_a, to_b = far_partials(table, features, block_weights)
    partial_code = dot(features, lowrank_in, NT)
    partial_back = dot(cotangent, lowrank_out, NT)
    partial_code, partial_back, later = lax.optimization_barrier((partial_code, partial_back, table))
    near = near_grads(later, items, features, cotangent)
    codes, backs = lax.psum((partial_code, partial_back), "wloop")
    codes = codes.astype(BF16)
    backs = backs.astype(BF16)
    near_share = lax.psum_scatter(near, "items", scatter_dimension=0, tiled=True)[0]
    to_a, to_b, from_a, from_b, codes, backs = lax.optimization_barrier(
        (to_a, to_b, from_a, from_b, codes, backs)
    )
    got_a = swapped(to_a, "wloop", top_bit - 2)
    got_b = swapped(to_b, "wloop", top_bit - 1)
    far = far_grads(items, features, cotangent, from_a, from_b, codes, backs)
    far, near_share = lax.optimization_barrier((far, near_share))
    far_share = lax.psum_scatter(far, "items", scatter_dimension=0, tiled=True)[0]
    total = near_total(table, features, block_weights, codes, lowrank_out)
    block_grads, grad_in, grad_out = place(table, near_share, far_share)
    mixed = (total + got_a.astype(F32) + got_b.astype(F32)).astype(BF16)
    return (mixed, block_grads, grad_in, grad_out)


def solution(mesh):
    return jax.shard_map(
        body,
        mesh=mesh,
        in_specs=(
            P(("groups", "items"), "wloop"),
            P(("groups", "items"), "wloop"),
            P("wloop", None, None),
            P("wloop"),
            P("wloop"),
            P(None, "wloop"),
            P(None, "wloop"),
        ),
        out_specs=(
            P(("groups", "items"), "wloop"),
            P(("groups", "items"), "wloop", None),
            P(("groups", "items"), "wloop"),
            P(("groups", "items"), "wloop"),
        ),
        check_vma=False,
    )
```
